512 devices in a mesh: dp: 32 (over z, y_hi), mp: 16 (over y_lo, x, core).
Axes of the slice: x: 4, y: 4 (y_hi: 2, y_lo: 2; y = y_hi * 2 + y_lo), z: 16, core: 2. Of those that a mesh axis runs over, the one named last changes fastest.
Arguments:
- activations: bfloat16 [16384, 4096], P('dp', 'mp'), may hold values from -6 to 6
- out_grads: bfloat16 [16384, 4096], P('dp', 'mp'), may hold values from -6 to 6
- valid_len: int32 [32], P('dp'), may hold values from 1 to 512, 12288 in all
- basis_act: bfloat16 [4096, 4096], P('dp', 'mp'), may hold values from -0.09375 to 0.09375
- basis_grad: bfloat16 [4096, 4096], P('dp', 'mp'), may hold values from -0.09375 to 0.09375
- eig_state: float32 [32, 2, 4096], P('dp', None, 'mp'), may hold values from 0.05 to 2
- owner_table: int32 [2], replicated, may hold values from 0 to 31, as said below
Outputs:
- precond_update: bfloat16 [4096, 4096], P(None, 'mp')
- new_state: float32 [32, 2, 4096], P('dp', None, 'mp')
The draws below stay inside these ranges and needn't reach their ends.
Inputs may be any that keep to these rules, and one draw needn't show every extreme that they name: `valid_len`: some shard has all 512 tokens valid. `owner_table`: the two owners are different ranks, and one of them is rank 32 - 1.
All inputs are finite; a program needn't handle non-finite values.
Results may differ from the reference program's by a relative error of at most 0.03.
Values may be sent and summed in bfloat16 or wider, within the bound.
No kernel may reach another device: no remote copies, remote signals or barrier semaphores. Data moves between devices by JAX's collectives and lax.ppermute only.
A program may use at most 64 MiB of HBM per device.

```python
import math
import jax
import jax.numpy as jnp
import numpy as np
from jax import lax

D = 4096
TOK_DEV = 512
TOKENS = 16384
N_DP = 32


def draw_owner_table(key, part):
    key = jax.random.fold_in(key, 7)
    other_key, order_key = jax.random.split(key)
    other = jax.random.randint(other_key, (), 0, N_DP - 1)
    last = jnp.int32(N_DP - 1)
    order = jax.random.randint(order_key, (), 0, 2)
    first = jnp.where(order == 0, last, other)
    second = jnp.where(order == 0, other, last)
    return jnp.stack([first, second]).astype(jnp.int32)


def level_of(key, extent, cuts, low, high):
    factor_of, own = 1.0, jax.random.fold_in(key, 6)
    for dim, parts in cuts:
        draws = jnp.exp(jax.random.uniform(jax.random.fold_in(own, dim), (parts,), jnp.float32, low / len(cuts), high / len(cuts)))
        factor_of = factor_of * jnp.repeat(draws, extent[dim] // parts).reshape([-1 if axis == dim else 1 for axis in range(len(extent))])
    return factor_of


def split_up(count, total, bound, slope):
    loads = [(1 << 20) // math.isqrt(standing ** slope) + 1 for standing in range(2, count + 1)]
    rest, counts = total - bound - (count - 1), [1] * (count - 1)
    while rest > 0:
        free = [i for i in range(count - 1) if counts[i] < bound]
        pool, left = sum([loads[i] for i in free]), rest
        for i in free:
            more = min(bound - counts[i], max(1, left * loads[i] // pool), rest)
            counts[i] = counts[i] + more
            rest = rest - more
    return np.array([bound] + counts)


def ragged(own_key, count, total, bound, slope):
    if count == 2:
        one = jax.random.randint(own_key, (), max(1, total - bound), min(bound, total - 1) + 1)
        return jnp.stack([one, total - one])
    tallies = jnp.asarray(split_up(count, total, bound, slope), jnp.int32)
    pairs = (count - 1) // 2
    donor, sink = tallies[1:1 + 2 * pairs:2], tallies[2:2 + 2 * pairs:2]
    room = jnp.minimum(donor - 1, bound - sink)
    shifted = jax.random.randint(jax.random.fold_in(own_key, 1), (pairs,), 0, 1 << 20) % (room + 1)
    tallies = tallies.at[1:1 + 2 * pairs:2].set(donor - shifted).at[2:2 + 2 * pairs:2].set(sink + shifted)
    return tallies[jax.random.permutation(jax.random.fold_in(own_key, 2), count)]


def bell_draw(rng, dims, spread, reach, cuts=(), held_as=jnp.bfloat16):
    result = spread * jax.random.normal(rng, dims, jnp.float32)
    if cuts:
        result = result * level_of(rng, dims, cuts, -0.22, 0.18)
    return jnp.clip(result, -reach, reach).astype(held_as)


def setup_inputs(seed: int = 0) -> dict:
    key_list = jax.random.split(jax.random.key(seed), 8)
    activations = bell_draw(key_list[0], (TOKENS, D), 1.0, 6.0, ((0, 32), (1, 16)))
    out_grads = bell_draw(key_list[1], (TOKENS, D), 1.0, 6.0, ((0, 32), (1, 16)))
    valid_len = ragged(key_list[2], N_DP, N_DP * TOK_DEV * 3 // 4, TOK_DEV, 1).astype(jnp.int32)
    basis_act = bell_draw(key_list[3], (D, D), D ** -0.5, 0.09375, ((0, 32), (1, 16)))
    basis_grad = bell_draw(key_list[4], (D, D), D ** -0.5, 0.09375, ((0, 32), (1, 16)))
    eig_state = jnp.clip(jnp.exp(math.log(2.0) - 3.6888794 * jax.random.uniform(key_list[5], (N_DP, 2, D), jnp.float32) ** level_of(key_list[5], (N_DP, 2, D), ((0, 32), (2, 16)), -0.2, 0.2)), 0.05, 2.0)
    owner_table = draw_owner_table(jax.random.fold_in(key_list[7], 71), 0)
    return dict(activations=activations, out_grads=out_grads, valid_len=valid_len, basis_act=basis_act, basis_grad=basis_grad, eig_state=eig_state, owner_table=owner_table)


EMA_WEIGHT = 0.5
DAMPING = 0.01

def reference(activations, out_grads, valid_len, basis_act, basis_grad, eig_state, owner_table):
    position = jnp.arange(TOKENS, dtype=jnp.int32)
    shard_index = (position // TOK_DEV).astype(jnp.int32)
    valid_mask = (position % TOK_DEV < valid_len[shard_index]).astype(jnp.float32)
    proj_act = jnp.dot(activations, basis_act, preferred_element_type=jnp.float32).astype(jnp.bfloat16)
    proj_grad = jnp.dot(out_grads, basis_grad, preferred_element_type=jnp.float32).astype(jnp.bfloat16)
    square_act = proj_act.astype(jnp.float32) * proj_act.astype(jnp.float32)
    square_grad = proj_grad.astype(jnp.float32) * proj_grad.astype(jnp.float32)
    stat_act = lax.optimization_barrier(jnp.sum(valid_mask[:, None] * square_act, axis=0)) / TOKENS
    stat_grad = lax.optimization_barrier(jnp.sum(valid_mask[:, None] * square_grad, axis=0)) / TOKENS
    eigen_act = EMA_WEIGHT * eig_state[owner_table[0], 0, :] + (1.0 - EMA_WEIGHT) * stat_act
    eigen_grad = EMA_WEIGHT * eig_state[owner_table[1], 1, :] + (1.0 - EMA_WEIGHT) * stat_grad
    new_state = jnp.broadcast_to(jnp.stack([eigen_act, eigen_grad])[None], (N_DP, 2, D))
    masked_act = jnp.where(valid_mask[:, None] > 0, proj_act, jnp.zeros_like(proj_act))
    grad_shards = proj_grad.reshape(TOKENS // TOK_DEV, TOK_DEV, D)
    act_shards = masked_act.reshape(TOKENS // TOK_DEV, TOK_DEV, D)

    def accumulate(running, shard_pair):
        grad_rows, act_rows = shard_pair
        shard_term = jnp.dot(grad_rows.T, act_rows, preferred_element_type=jnp.float32).astype(jnp.bfloat16)
        shard_term = lax.optimization_barrier(shard_term)
        return (running + shard_term.astype(jnp.float32), None)
    running, unused = lax.scan(accumulate, jnp.zeros((D, D), jnp.float32), (grad_shards, act_shards))
    rotated = running / math.sqrt(TOKENS)
    denom = eigen_grad[:, None] * eigen_act[None, :] + DAMPING
    precond_update = (rotated / denom).astype(jnp.bfloat16)
    return (precond_update, new_state)
```

```python
import functools
import math

import jax
import jax.numpy as jnp
from jax import lax
from jax.experimental import pallas as pl
from jax.experimental.pallas import tpu as pltpu
from jax.sharding import Mesh, PartitionSpec as P

EMA_WEIGHT = 0.5
DAMPING = 0.01
DP = ("z", "h")
MP = ("l", "x", "c")
BF16 = jnp.bfloat16
F32 = jnp.float32


def swap(array, axis):
    return lax.ppermute(array, axis, [(0, 1), (1, 0)])


def turn(array, axis, by):
    size = lax.axis_size(axis)
    return lax.ppermute(array, axis, [(i, (i + by) % size) for i in range(size)])


def project_kernel(scalars, own, other, basis, act_out, grad_out, stat_out, acc_act, acc_grad):
    step = pl.program_id(0)
    core = scalars[0]
    width = act_out.shape[1]

    @pl.when(step == 0)
    def _():
        acc_act[...] = jnp.zeros_like(acc_act)
        acc_grad[...] = jnp.zeros_like(acc_grad)

    def mul(a, b):
        return jnp.dot(a, b, preferred_element_type=F32)

    mine, theirs = basis[core], basis[1 - core]
    acc_act[...] += mul(own[0, 0], mine[:, :width]) + mul(other[0, 0], theirs[:, :width])
    acc_grad[...] += mul(own[0, 1], mine[:, width:]) + mul(other[0, 1], theirs[:, width:])

    @pl.when(step == pl.num_programs(0) - 1)
    def _():
        rows = lax.broadcasted_iota(jnp.int32, acc_act.shape, 0)
        valid = rows < scalars[1]
        act = jnp.where(valid, acc_act[...].astype(BF16).astype(F32), 0.0)
        grad = acc_grad[...].astype(BF16)
        wide = jnp.where(valid, grad.astype(F32), 0.0)
        act_out[...] = act.astype(BF16)
        grad_out[...] = grad
        stat_out[0:1] = jnp.sum(act * act, axis=0, keepdims=True)
        stat_out[1:2] = jnp.sum(wide * wide, axis=0, keepdims=True)


def project(scalars, own, other, basis):
    steps, _, tokens, depth = own.shape
    width = basis.shape[-1] // 2
    blocks = pl.BlockSpec((1, 2, tokens, depth), lambda k, s: (k, 0, 0, 0))
    return pl.pallas_call(
        project_kernel,
        grid_spec=pltpu.PrefetchScalarGridSpec(
            num_scalar_prefetch=1,
            grid=(steps,),
            in_specs=[blocks, blocks, pl.BlockSpec((2, depth, 2 * width), lambda k, s: (k, 0, 0))],
            out_specs=[
                pl.BlockSpec((tokens, width), lambda k, s: (0, 0)),
                pl.BlockSpec((tokens, width), lambda k, s: (0, 0)),
                pl.BlockSpec((2, width), lambda k, s: (0, 0)),
            ],
            scratch_shapes=[pltpu.VMEM((tokens, width), F32)] * 2,
        ),
        out_shape=[
            jax.ShapeDtypeStruct((tokens, width), BF16),
            jax.ShapeDtypeStruct((tokens, width), BF16),
            jax.ShapeDtypeStruct((2, width), F32),
        ],
        compiler_params=pltpu.CompilerParams(vmem_limit_bytes=32 << 20),
        cost_estimate=pl.CostEstimate(flops=4 * steps * 4 * tokens * depth * width, bytes_accessed=14 << 20, transcendentals=0),
    )(scalars, own, other, basis)


def term_kernel(scalars, *refs):
    grads, acts, out = refs[:4], refs[4:8], refs[8]
    parts, rows, width = out.shape[0] // 4, out.shape[2], out.shape[3]
    for g in range(4):
        block = scalars[g]
        for a in range(4):
            tile = lax.dot_general(grads[g][...], acts[a][...], (((0,), (0,)), ((), ())), preferred_element_type=F32)
            tile = tile.astype(BF16).reshape(parts, rows, width)
            for p in range(parts):
                out[block * parts + p, scalars[4 + a]] = tile[p]


def term(scalars, grads, acts, chunks):
    tokens, width = acts[0].shape
    rows = 4 * width // chunks
    whole = pl.BlockSpec(memory_space=pltpu.VMEM)
    return pl.pallas_call(
        term_kernel,
        in_specs=[pl.BlockSpec(memory_space=pltpu.SMEM)] + [whole] * 8,
        out_specs=whole,
        out_shape=jax.ShapeDtypeStruct((chunks, 4, rows, width), BF16),
        compiler_params=pltpu.CompilerParams(vmem_limit_bytes=32 << 20),
        cost_estimate=pl.CostEstimate(flops=32 * tokens * width * width, bytes_accessed=4 << 20, transcendentals=0),
    )(scalars, *grads, *acts)


def local(activations, out_grads, valid_len, basis_act, basis_grad, eig_state, owner_table):
    z, h, l, x, c = (lax.axis_index(a) for a in ("z", "h", "l", "x", "c"))
    chunks = lax.axis_size("z")
    tokens, width = activations.shape
    token_total = tokens * chunks * lax.axis_size("h")

    bases = jnp.concatenate([basis_act, basis_grad], axis=1)
    paired = swap(bases, "h")
    bases = jnp.concatenate([jnp.where(h == 0, bases, paired), jnp.where(h == 0, paired, bases)], axis=0)
    inputs = jnp.stack([activations, out_grads])
    bases, inputs = lax.optimization_barrier((bases, inputs))
    all_bases = lax.all_gather(bases, "z", axis=0)
    own = lax.all_to_all(jnp.broadcast_to(inputs[None], (8, *inputs.shape)), ("l", "x"), 0, 0)
    other = swap(own, "c")

    scalars = jnp.stack([c, valid_len[0]]).astype(jnp.int32)
    act, grad, stat = project(scalars, own, other, all_bases)

    acts = [act, turn(act, "x", 1), turn(act, "x", -1), turn(act, "x", 2)]
    far = swap(grad, "l")
    grads = [grad, far, swap(grad, "c"), swap(far, "c")]
    q = 2 * l + c
    places = jnp.stack([q, q ^ 2, q ^ 1, q ^ 3, x, (x - 1) % 4, (x + 1) % 4, (x + 2) % 4]).astype(jnp.int32)
    partial_term = term(places, grads, acts, chunks)
    summed = lax.psum_scatter(partial_term, "z", scatter_dimension=0, tiled=True)[0]

    rank = z * 2 + h
    mine = (owner_table == rank).astype(F32)
    part = (1.0 - EMA_WEIGHT) * (stat / token_total) + EMA_WEIGHT * mine[:, None] * eig_state[0]
    part = lax.psum(part, "z")
    eigen = part + swap(part, "h")
    new_state = eigen[None]
    eigen_rows = lax.all_gather(eigen[1], MP, axis=0).reshape(2, 4, 2, width)
    eigen_rows = lax.dynamic_index_in_dim(eigen_rows, z // 8, 0, keepdims=False)
    eigen_rows = lax.dynamic_index_in_dim(eigen_rows, (z // 4) % 2, 1, keepdims=False)
    rows = partial_term.shape[2]
    eigen_rows = lax.dynamic_slice_in_dim(eigen_rows, (z % 4) * rows, rows, axis=1)

    moved = lax.all_to_all(jnp.broadcast_to(summed[None], (2, *summed.shape)).reshape(8, rows, width), ("h", "x"), 0, 0)
    moved = moved.reshape(2, 4, rows, width).astype(F32)
    denom = eigen_rows[:, :, None] * eigen[0][None, None, :] + DAMPING
    values = (moved[0] + moved[1]) / math.sqrt(token_total) / denom

    top = jnp.max(jnp.abs(values))
    power = jnp.where(top > 0, jnp.clip(jnp.floor(14.0 - jnp.log2(top)), -100.0, 126.0), 0.0)
    sent = jnp.concatenate(
        [(values * jnp.exp2(power)).astype(jnp.float16).reshape(4 * rows, width), jnp.full((16, width), power, jnp.float16)],
        axis=0,
    )
    got = lax.all_gather(sent, "z", axis=0)
    back = jnp.exp2(-got[:, 4 * rows, 0].astype(F32))
    full = got[:, : 4 * rows].astype(F32) * back[:, None, None]
    full = full.astype(BF16).reshape(2, 2, 4, 4, rows, width).transpose(0, 3, 1, 2, 4, 5)
    return (full.reshape(chunks * 4 * rows, width), new_state)


def solution(mesh):
    fine = Mesh(mesh.devices.reshape(16, 2, 2, 4, 2), ("z", "h", "l", "x", "c"))
    placed = (P(DP, MP), P(DP, MP), P(DP), P(DP, MP), P(DP, MP), P(DP, None, MP), P())
    return jax.shard_map(
        local, mesh=fine, in_specs=placed, out_specs=(P(None, MP), P(DP, None, MP)), check_vma=False
    )
```

```python
import functools
import math

import jax
import jax.numpy as jnp
from jax import lax
from jax.experimental import pallas as pl
from jax.experimental.pallas import tpu as pltpu
from jax.sharding import Mesh, PartitionSpec as P

EMA_WEIGHT = 0.5
DAMPING = 0.01
Z = ("z1", "z0")
DP = ("z1", "z0", "h")
MP = ("l", "x", "c")
BF16 = jnp.bfloat16
F32 = jnp.float32


def swap(array, axis):
    return lax.ppermute(array, axis, [(0, 1), (1, 0)])


def project_kernel(limit, inputs, basis, proj_out, stat_out, total, *, masked):
    step = pl.program_id(0)

    @pl.when(step == 0)
    def _():
        total[...] = jnp.zeros_like(total)

    depth, width = inputs.shape[-1], basis.shape[-1]
    total[...] += sum(
        jnp.dot(inputs[i, 0], basis[i].reshape(depth, width), preferred_element_type=F32) for i in range(inputs.shape[0])
    )

    @pl.when(step == pl.num_programs(0) - 1)
    def _():
        rounded = total[...].astype(BF16)
        valid = lax.broadcasted_iota(jnp.int32, total.shape, 0) < limit[0]
        kept = jnp.where(valid, rounded.astype(F32), 0.0)
        stat_out[...] = jnp.sum(kept * kept, axis=0, keepdims=True)
        for i in range(proj_out.shape[0]):
            proj_out[i] = kept.astype(BF16) if masked else rounded


def project(limit, inputs, side, basis, masked, copies):
    parts, _, tokens, depth = inputs.shape
    width = basis.shape[-1]
    group = 4
    return pl.pallas_call(
        functools.partial(project_kernel, masked=masked),
        grid_spec=pltpu.PrefetchScalarGridSpec(
            num_scalar_prefetch=1,
            grid=(parts // group,),
            in_specs=[
                pl.BlockSpec((group, 1, tokens, depth), lambda k, s: (k, side, 0, 0)),
                pl.BlockSpec((group, 2, depth // 2, width), lambda k, s: (k, 0, 0, 0)),
            ],
            out_specs=[
                pl.BlockSpec((copies, tokens, width), lambda k, s: (0, 0, 0)),
                pl.BlockSpec((1, width), lambda k, s: (0, 0)),
            ],
            scratch_shapes=[pltpu.VMEM((tokens, width), F32)],
        ),
        out_shape=[
            jax.ShapeDtypeStruct((copies, tokens, width), BF16),
            jax.ShapeDtypeStruct((1, width), F32),
        ],
        compiler_params=pltpu.CompilerParams(vmem_limit_bytes=60 << 20),
        cost_estimate=pl.CostEstimate(flops=2 * parts * tokens * depth * width, bytes_accessed=7 << 20, transcendentals=0),
    )(limit, inputs, basis)


def pack(values):
    values = values.astype(F32)
    parts, rows, width = values.shape
    top = jnp.max(jnp.abs(values), axis=1)
    power = jnp.where(top > 0, jnp.clip(jnp.floor(14.0 - jnp.log2(top)), -100.0, 126.0), 0.0)
    scaled = (values * jnp.exp2(power)[:, None]).astype(jnp.float16).reshape(parts * rows, width)
    return jnp.concatenate([scaled, jnp.pad(power.astype(jnp.float16), ((0, 8 - parts), (0, 0)))], axis=0)


def unpack(packed, parts):
    rows = packed.shape[-2] - 8
    part = rows // parts

    def one(i):
        back = jnp.exp2(-packed[..., rows + i : rows + i + 1, :].astype(F32))
        return (packed[..., i * part : (i + 1) * part, :].astype(F32) * back).astype(BF16)

    return [one(i) for i in range(parts)]


def term_kernel(places, *refs):
    grads, acts, out = refs[:4], refs[4], refs[5]
    rows, width = out.shape[3:]
    parts = width // rows
    for g in range(4):
        first = places[g] * (parts // 2)
        for a in range(4):
            tile = lax.dot_general(grads[g][0], acts[a], (((0,), (0,)), ((), ())), preferred_element_type=F32)
            tile = tile.astype(BF16).reshape(parts, rows, width)
            for p in range(parts):
                out[first + p // 2, p % 2, a] = tile[p]


def term(places, grads, acts, chunks):
    _, tokens, width = acts.shape
    whole = pl.BlockSpec(memory_space=pltpu.VMEM)
    return pl.pallas_call(
        term_kernel,
        in_specs=[pl.BlockSpec(memory_space=pltpu.SMEM)] + [whole] * 5,
        out_specs=whole,
        out_shape=jax.ShapeDtypeStruct((chunks // 2, 2, 4, 4 * width // chunks, width), BF16),
        compiler_params=pltpu.CompilerParams(vmem_limit_bytes=32 << 20),
        cost_estimate=pl.CostEstimate(flops=32 * tokens * width * width, bytes_accessed=4 << 20, transcendentals=0),
    )(places, *grads, acts)


def local(activations, out_grads, valid_len, basis_act, basis_grad, eig_state, owner_table):
    z, h, l, x, c = (lax.axis_index(a) for a in (Z, "h", "l", "x", "c"))
    chunks = lax.axis_size(Z)
    tokens, width = activations.shape
    token_total = tokens * chunks * lax.axis_size("h")

    bases = pack(jnp.stack([basis_act, basis_grad]))
    activations, out_grads, bases = lax.optimization_barrier((activations, out_grads, bases))
    paired = swap(bases, "h")
    all_inputs = lax.all_gather(jnp.stack([activations, out_grads]), MP, axis=0)
    bases = jnp.stack([jnp.where(h == 0, bases, paired), jnp.where(h == 0, paired, bases)])
    bases = lax.all_gather(bases, Z, axis=0)
    whole_act, whole_grad = unpack(bases, 2)

    act, stat_act = project(valid_len, all_inputs, 0, whole_act, True, 4)
    acts = lax.all_to_all(act, "x", 0, 0)
    grad, stat_grad = project(valid_len, all_inputs, 1, whole_grad, False, 1)
    far = swap(grad, "l")
    grads = [grad, far, swap(grad, "c"), swap(far, "c")]
    q = 2 * l + c
    places = jnp.stack([q, q ^ 2, q ^ 1, q ^ 3]).astype(jnp.int32)
    partial_term = term(places, grads, acts, chunks)
    stat = jnp.concatenate([stat_act, stat_grad], axis=0)
    partial_term, stat = lax.optimization_barrier((partial_term, stat))
    summed = lax.psum_scatter(partial_term, "z1", scatter_dimension=0, tiled=True)[0]

    rank = z * 2 + h
    mine = (owner_table == rank).astype(F32)
    part = (1.0 - EMA_WEIGHT) * (stat / token_total) + EMA_WEIGHT * mine[:, None] * eig_state[0]
    part = lax.psum(part, Z)
    eigen = part + swap(part, "h")
    new_state = eigen[None]
    eigen_rows = lax.all_gather(eigen[1], MP, axis=0).reshape(2, 4, 2, width)
    eigen_rows = lax.dynamic_index_in_dim(eigen_rows, z >> 3, 0, keepdims=False)
    eigen_rows = lax.dynamic_index_in_dim(eigen_rows, (z >> 2) & 1, 1, keepdims=False)
    rows = partial_term.shape[3]
    eigen_rows = lax.dynamic_slice_in_dim(eigen_rows, (z & 3) * rows, rows, axis=1)

    summed, eigen_rows = lax.optimization_barrier((summed, eigen_rows))
    moved = jnp.broadcast_to(summed[:, None], (2, 2, 4, rows, width)).reshape(16, rows, width)
    moved = lax.all_to_all(moved, ("z0", "h", "x"), 0, 0).reshape(4, 4, rows, width).astype(F32)
    denom = eigen_rows[:, :, None] * eigen[0][None, None, :] + DAMPING
    values = jnp.sum(moved, axis=0) / math.sqrt(token_total) / denom
    (full,) = unpack(lax.all_gather(pack(values.reshape(1, 4 * rows, width)), Z, axis=0), 1)
    full = full.reshape(2, 2, 4, 4, rows, width).transpose(0, 3, 1, 2, 4, 5)
    return (full.reshape(chunks * 4 * rows, width), new_state)


def solution(mesh):
    fine = Mesh(mesh.devices.reshape(8, 2, 2, 2, 4, 2), ("z1", "z0", "h", "l", "x", "c"))
    placed = (P(DP, MP), P(DP, MP), P(DP), P(DP, MP), P(DP, MP), P(DP, None, MP), P())
    return jax.shard_map(
        local, mesh=fine, in_specs=placed, out_specs=(P(None, MP), P(DP, None, MP)), check_vma=False
    )
```

```python
import functools
import math

import jax
import jax.numpy as jnp
from jax import lax
from jax.experimental import pallas as pl
from jax.experimental.pallas import tpu as pltpu
from jax.sharding import Mesh, PartitionSpec as P

EMA_WEIGHT = 0.5
DAMPING = 0.01
Z = ("z1", "z0")
DP = ("z1", "z0", "h")
MP = ("l", "x", "c")
BF16 = jnp.bfloat16
F32 = jnp.float32


def swap(array, axis):
    return lax.ppermute(array, axis, [(0, 1), (1, 0)])


def project_kernel(limit, inputs, basis, proj_out, stat_out, total, *, masked):
    step = pl.program_id(0)

    @pl.when(step == 0)
    def _():
        total[...] = jnp.zeros_like(total)

    depth, width = inputs.shape[-1], basis.shape[-1]
    total[...] += sum(
        jnp.dot(inputs[i, 0], basis[i].reshape(depth, width), preferred_element_type=F32) for i in range(inputs.shape[0])
    )

    @pl.when(step == pl.num_programs(0) - 1)
    def _():
        rounded = total[...].astype(BF16)
        valid = lax.broadcasted_iota(jnp.int32, total.shape, 0) < limit[0]
        kept = jnp.where(valid, rounded.astype(F32), 0.0)
        stat_out[...] = jnp.sum(kept * kept, axis=0, keepdims=True)
        for i in range(proj_out.shape[0]):
            proj_out[i] = kept.astype(BF16) if masked else rounded


def project(limit, inputs, side, basis, masked, copies):
    parts, _, tokens, depth = inputs.shape
    width = basis.shape[-1]
    group = 8
    return pl.pallas_call(
        functools.partial(project_kernel, masked=masked),
        grid_spec=pltpu.PrefetchScalarGridSpec(
            num_scalar_prefetch=1,
            grid=(parts // group,),
            in_specs=[
                pl.BlockSpec((group, 1, tokens, depth), lambda k, s: (k, side, 0, 0)),
                pl.BlockSpec((group, 2, depth // 2, width), lambda k, s: (k, 0, 0, 0)),
            ],
            out_specs=[
                pl.BlockSpec((copies, tokens, width), lambda k, s: (0, 0, 0)),
                pl.BlockSpec((1, width), lambda k, s: (0, 0)),
            ],
            scratch_shapes=[pltpu.VMEM((tokens, width), F32)],
        ),
        out_shape=[
            jax.ShapeDtypeStruct((copies, tokens, width), BF16),
            jax.ShapeDtypeStruct((1, width), F32),
        ],
        compiler_params=pltpu.CompilerParams(vmem_limit_bytes=48 << 20),
        cost_estimate=pl.CostEstimate(flops=2 * parts * tokens * depth * width, bytes_accessed=7 << 20, transcendentals=0),
    )(limit, inputs, basis)


def pack(values):
    values = values.astype(F32)
    parts, rows, width = values.shape
    top = jnp.max(jnp.abs(values), axis=1)
    power = jnp.where(top > 0, jnp.clip(jnp.floor(14.0 - jnp.log2(top)), -100.0, 126.0), 0.0)
    scaled = (values * jnp.exp2(power)[:, None]).astype(jnp.float16).reshape(parts * rows, width)
    return jnp.concatenate([scaled, jnp.pad(power.astype(jnp.float16), ((0, 8 - parts), (0, 0)))], axis=0)


def unpack(packed, parts):
    rows = packed.shape[-2] - 8
    part = rows // parts

    def one(i):
        back = jnp.exp2(-packed[..., rows + i : rows + i + 1, :].astype(F32))
        return (packed[..., i * part : (i + 1) * part, :].astype(F32) * back).astype(BF16)

    return [one(i) for i in range(parts)]


def term_kernel(places, *refs):
    grads, acts, out = refs[:4], refs[4], refs[5]
    rows, width = out.shape[3:]
    parts = width // rows
    for g in range(4):
        first = places[g] * (parts // 2)
        for a in range(4):
            tile = lax.dot_general(grads[g][0], acts[a], (((0,), (0,)), ((), ())), preferred_element_type=F32)
            tile = tile.astype(BF16).reshape(parts, rows, width)
            for p in range(parts):
                out[first + p // 2, p % 2, a] = tile[p]


def term(places, grads, acts, chunks):
    _, tokens, width = acts.shape
    whole = pl.BlockSpec(memory_space=pltpu.VMEM)
    return pl.pallas_call(
        term_kernel,
        in_specs=[pl.BlockSpec(memory_space=pltpu.SMEM)] + [whole] * 5,
        out_specs=whole,
        out_shape=jax.ShapeDtypeStruct((chunks // 2, 2, 4, 4 * width // chunks, width), BF16),
        compiler_params=pltpu.CompilerParams(vmem_limit_bytes=32 << 20),
        cost_estimate=pl.CostEstimate(flops=32 * tokens * width * width, bytes_accessed=4 << 20, transcendentals=0),
    )(places, *grads, acts)


def local(activations, out_grads, valid_len, basis_act, basis_grad, eig_state, owner_table):
    z, h, l, x, c = (lax.axis_index(a) for a in (Z, "h", "l", "x", "c"))
    chunks = lax.axis_size(Z)
    tokens, width = activations.shape
    token_total = tokens * chunks * lax.axis_size("h")

    bases = pack(jnp.stack([basis_act, basis_grad]))
    activations, out_grads, bases = lax.optimization_barrier((activations, out_grads, bases))
    paired = swap(bases, "h")
    all_inputs = lax.all_gather(jnp.stack([activations, out_grads]), MP, axis=0)
    bases = jnp.concatenate([jnp.where(h == 0, bases, paired), jnp.where(h == 0, paired, bases)], axis=0)
    bases = lax.all_gather(bases, Z, axis=0).reshape(chunks, 2, *paired.shape)
    whole_act, whole_grad = unpack(bases, 2)

    act, stat_act = project(valid_len, all_inputs, 0, whole_act, True, 4)
    acts = lax.all_to_all(act, "x", 0, 0)
    grad, stat_grad = project(valid_len, all_inputs, 1, whole_grad, False, 1)
    far = swap(grad, "l")
    grads = [grad, far, swap(grad, "c"), swap(far, "c")]
    q = 2 * l + c
    places = jnp.stack([q, q ^ 2, q ^ 1, q ^ 3]).astype(jnp.int32)
    partial_term = term(places, grads, acts, chunks)
    stat = jnp.concatenate([stat_act, stat_grad], axis=0)
    partial_term, stat = lax.optimization_barrier((partial_term, stat))
    rows = partial_term.shape[3]
    summed = lax.psum_scatter(partial_term.reshape(-1, width), "z1", scatter_dimension=0, tiled=True)
    summed = summed.reshape(2, 4, rows, width)

    rank = z * 2 + h
    mine = (owner_table == rank).astype(F32)
    part = (1.0 - EMA_WEIGHT) * (stat / token_total) + EMA_WEIGHT * mine[:, None] * eig_state[0]
    part = lax.psum(part, Z)
    eigen = part + swap(part, "h")
    new_state = eigen[None]
    eigen_rows = lax.all_to_all(jnp.broadcast_to(eigen[1], (16, 1, width)), MP, 0, 0).reshape(2, 4, 2, width)
    eigen_rows = lax.dynamic_index_in_dim(eigen_rows, z >> 3, 0, keepdims=False)
    eigen_rows = lax.dynamic_index_in_dim(eigen_rows, (z >> 2) & 1, 1, keepdims=False)
    eigen_rows = lax.dynamic_slice_in_dim(eigen_rows, (z & 3) * rows, rows, axis=1)

    summed, eigen_rows = lax.optimization_barrier((summed, eigen_rows))
    moved = jnp.broadcast_to(summed[:, None], (2, 2, 4, rows, width)).reshape(16, rows, width)
    moved = lax.all_to_all(moved, ("z0", "h", "x"), 0, 0).reshape(4, 4, rows, width).astype(F32)
    denom = eigen_rows[:, :, None] * eigen[0][None, None, :] + DAMPING
    values = jnp.sum(moved, axis=0) / math.sqrt(token_total) / denom
    (full,) = unpack(lax.all_gather(pack(values.reshape(1, 4 * rows, width)), Z, axis=0), 1)
    full = full.reshape(2, 2, 4, 4, rows, width).transpose(0, 3, 1, 2, 4, 5)
    return (full.reshape(chunks * 4 * rows, width), new_state)


def solution(mesh):
    fine = Mesh(mesh.devices.reshape(8, 2, 2, 2, 4, 2), ("z1", "z0", "h", "l", "x", "c"))
    placed = (P(DP, MP), P(DP, MP), P(DP), P(DP, MP), P(DP, MP), P(DP, None, MP), P())
    return jax.shard_map(
        local, mesh=fine, in_specs=placed, out_specs=(P(None, MP), P(DP, None, MP)), check_vma=False
    )
```

```python
import functools
import math

import jax
import jax.numpy as jnp
from jax import lax
from jax.experimental import pallas as pl
from jax.experimental.pallas import tpu as pltpu
from jax.sharding import Mesh, PartitionSpec as P

EMA_WEIGHT = 0.5
DAMPING = 0.01
Z = ("z1", "z0")
DP = ("z1", "z0", "h")
MP = ("l", "x", "c")
BF16 = jnp.bfloat16
F32 = jnp.float32


def swap(array, axis):
    return lax.ppermute(array, axis, [(0, 1), (1, 0)])


def project_kernel(limit, inputs, basis, proj_out, stat_out, total, *, masked):
    step = pl.program_id(0)

    @pl.when(step == 0)
    def _():
        total[...] = jnp.zeros_like(total)

    depth, width = inputs.shape[-1], basis.shape[-1]
    total[...] += sum(
        jnp.dot(inputs[i, 0], basis[i].reshape(depth, width), preferred_element_type=F32) for i in range(inputs.shape[0])
    )

    @pl.when(step == pl.num_programs(0) - 1)
    def _():
        rounded = total[...].astype(BF16)
        valid = lax.broadcasted_iota(jnp.int32, total.shape, 0) < limit[0]
        kept = jnp.where(valid, rounded.astype(F32), 0.0)
        stat_out[...] = jnp.sum(kept * kept, axis=0, keepdims=True)
        for i in range(proj_out.shape[0]):
            proj_out[i] = kept.astype(BF16) if masked else rounded


def project(limit, inputs, side, basis, masked, copies):
    parts, _, tokens, depth = inputs.shape
    width = basis.shape[-1]
    group = 8
    return pl.pallas_call(
        functools.partial(project_kernel, masked=masked),
        grid_spec=pltpu.PrefetchScalarGridSpec(
            num_scalar_prefetch=1,
            grid=(parts // group,),
            in_specs=[
                pl.BlockSpec((group, 1, tokens, depth), lambda k, s: (k, side, 0, 0)),
                pl.BlockSpec((group, 2, depth // 2, width), lambda k, s: (k, 0, 0, 0)),
            ],
            out_specs=[
                pl.BlockSpec((copies, tokens, width), lambda k, s: (0, 0, 0)),
                pl.BlockSpec((1, width), lambda k, s: (0, 0)),
            ],
            scratch_shapes=[pltpu.VMEM((tokens, width), F32)],
        ),
        out_shape=[
            jax.ShapeDtypeStruct((copies, tokens, width), BF16),
            jax.ShapeDtypeStruct((1, width), F32),
        ],
        compiler_params=pltpu.CompilerParams(vmem_limit_bytes=44 << 20),
        cost_estimate=pl.CostEstimate(flops=2 * parts * tokens * depth * width, bytes_accessed=7 << 20, transcendentals=0),
    )(limit, inputs, basis)


def pack(values):
    values = values.astype(F32)
    parts, rows, width = values.shape
    top = jnp.max(jnp.abs(values), axis=1)
    power = jnp.where(top > 0, jnp.clip(jnp.floor(14.0 - jnp.log2(top)), -100.0, 126.0), 0.0)
    scaled = (values * jnp.exp2(power)[:, None]).astype(jnp.float16).reshape(parts * rows, width)
    return jnp.concatenate([scaled, jnp.pad(power.astype(jnp.float16), ((0, 8 - parts), (0, 0)))], axis=0)


def unpack(packed, parts):
    rows = packed.shape[-2] - 8
    part = rows // parts

    def one(i):
        back = jnp.exp2(-packed[..., rows + i : rows + i + 1, :].astype(F32))
        return (packed[..., i * part : (i + 1) * part, :].astype(F32) * back).astype(BF16)

    return [one(i) for i in range(parts)]


def term_kernel(places, *refs):
    grads, acts, out = refs[:4], refs[4], refs[5]
    rows, width = out.shape[3:]
    parts = width // rows
    for g in range(4):
        first = places[g] * (parts // 2)
        for a in range(4):
            tile = lax.dot_general(grads[g][0], acts[a], (((0,), (0,)), ((), ())), preferred_element_type=F32)
            tile = tile.astype(BF16).reshape(parts, rows, width)
            for p in range(parts):
                out[first + p // 2, p % 2, a] = tile[p]


def term(places, grads, acts, chunks):
    _, tokens, width = acts.shape
    whole = pl.BlockSpec(memory_space=pltpu.VMEM)
    return pl.pallas_call(
        term_kernel,
        in_specs=[pl.BlockSpec(memory_space=pltpu.SMEM)] + [whole] * 5,
        out_specs=whole,
        out_shape=jax.ShapeDtypeStruct((chunks // 2, 2, 4, 4 * width // chunks, width), BF16),
        compiler_params=pltpu.CompilerParams(vmem_limit_bytes=32 << 20),
        cost_estimate=pl.CostEstimate(flops=32 * tokens * width * width, bytes_accessed=4 << 20, transcendentals=0),
    )(places, *grads, acts)


def local(activations, out_grads, valid_len, basis_act, basis_grad, eig_state, owner_table):
    z, h, l, x, c = (lax.axis_index(a) for a in (Z, "h", "l", "x", "c"))
    chunks = lax.axis_size(Z)
    tokens, width = activations.shape
    token_total = tokens * chunks * lax.axis_size("h")

    bases = pack(jnp.stack([basis_act, basis_grad]))
    activations, out_grads, bases = lax.optimization_barrier((activations, out_grads, bases))
    paired = swap(bases, "h")
    all_inputs = lax.all_gather(jnp.stack([activations, out_grads]), MP, axis=0)
    bases = jnp.concatenate([jnp.where(h == 0, bases, paired), jnp.where(h == 0, paired, bases)], axis=0)
    bases = lax.all_gather(bases, Z, axis=0).reshape(chunks, 2, *paired.shape)
    whole_act, whole_grad = unpack(bases, 2)

    act, stat_act = project(valid_len, all_inputs, 0, whole_act, True, 4)
    acts = lax.all_to_all(act, "x", 0, 0)
    grad, stat_grad = project(valid_len, all_inputs, 1, whole_grad, False, 1)
    far = swap(grad, "l")
    grads = [grad, far, swap(grad, "c"), swap(far, "c")]
    q = 2 * l + c
    places = jnp.stack([q, q ^ 2, q ^ 1, q ^ 3]).astype(jnp.int32)
    partial_term = term(places, grads, acts, chunks)
    stat = jnp.concatenate([stat_act, stat_grad], axis=0)
    partial_term, stat = lax.optimization_barrier((partial_term, stat))
    rows = partial_term.shape[3]
    summed = lax.psum_scatter(partial_term.reshape(-1, width), "z1", scatter_dimension=0, tiled=True)
    summed = summed.reshape(2, 4, rows, width)

    rank = z * 2 + h
    mine = (owner_table == rank).astype(F32)
    part = (1.0 - EMA_WEIGHT) * (stat / token_total) + EMA_WEIGHT * mine[:, None] * eig_state[0]
    part = lax.psum(part, Z)
    eigen = part + swap(part, "h")
    new_state = eigen[None]
    eigen_rows = lax.all_to_all(jnp.broadcast_to(eigen[1], (16, 1, width)), MP, 0, 0).reshape(2, 4, 2, width)
    eigen_rows = lax.dynamic_index_in_dim(eigen_rows, z >> 3, 0, keepdims=False)
    eigen_rows = lax.dynamic_index_in_dim(eigen_rows, (z >> 2) & 1, 1, keepdims=False)
    eigen_rows = lax.dynamic_slice_in_dim(eigen_rows, (z & 3) * rows, rows, axis=1)

    summed, eigen_rows = lax.optimization_barrier((summed, eigen_rows))
    moved = jnp.broadcast_to(summed[:, None], (2, 2, 4, rows, width)).reshape(16, rows, width)
    moved = lax.all_to_all(moved, ("z0", "h", "x"), 0, 0).reshape(4, 4, rows, width).astype(F32)
    denom = eigen_rows[:, :, None] * eigen[0][None, None, :] + DAMPING
    values = jnp.sum(moved, axis=0) / math.sqrt(token_total) / denom
    (full,) = unpack(lax.all_gather(pack(values.reshape(1, 4 * rows, width)), Z, axis=0), 1)
    full = full.reshape(2, 2, 4, 4, rows, width).transpose(0, 3, 1, 2, 4, 5)
    return (full.reshape(chunks * 4 * rows, width), new_state)


def solution(mesh):
    fine = Mesh(mesh.devices.reshape(8, 2, 2, 2, 4, 2), ("z1", "z0", "h", "l", "x", "c"))
    placed = (P(DP, MP), P(DP, MP), P(DP), P(DP, MP), P(DP, MP), P(DP, None, MP), P())
    return jax.shard_map(
        local, mesh=fine, in_specs=placed, out_specs=(P(None, MP), P(DP, None, MP)), check_vma=False
    )
```
